256 devices in a mesh: row: 16 (over z, y_lo), col: 16 (over y_hi, x, core).
Axes of the slice: x: 4, y: 4 (y_hi: 2, y_lo: 2; y = y_hi * 2 + y_lo), z: 8, core: 2. Of those that a mesh axis runs over, the one named last changes fastest.
Arguments:
- features: bfloat16 [2048, 6144], P('col', 'row'), may hold values from -8 to 8
- w_in: bfloat16 [6144, 24576], P('row', 'col'), may hold values from -0.078125 to 0.078125
- b_in: float32 [24576], P('col'), may hold values from -3 to 3
- w_out: bfloat16 [24576, 6144], P('col', 'row'), may hold values from -0.0390625 to 0.0390625
- b_out: float32 [6144], P('row'), may hold values from -3 to 3
- grad_out: bfloat16 [2048, 6144], P('col', 'row'), may hold values from -6 to 6
Outputs:
- branch_out: bfloat16 [2048, 6144], P('col', 'row')
- grad_features: bfloat16 [2048, 6144], P('col', 'row')
- grad_w_in: float32 [6144, 24576], P('row', 'col')
- grad_b_in: float32 [24576], P('col')
- grad_w_out: float32 [24576, 6144], P('col', 'row')
- grad_b_out: float32 [6144], P('row')
The draws below stay inside these ranges and needn't reach their ends.
All inputs are finite; a program needn't handle non-finite values.
Results may differ from the reference program's by a relative error of at most 0.039.
Values may be sent and summed in bfloat16 or wider, within the bound.
No kernel may reach another device: no remote copies, remote signals or barrier semaphores. Data moves between devices by JAX's collectives and lax.ppermute only.
A program may use at most 128 MiB of HBM per device.

```python
import math
import jax
import jax.numpy as jnp
from jax import lax

D = 6144
FF = 24576
TOKENS = 2048
N_ROW = 16
N_COL = 16


def strengthened(array, rng, source, target, parts, factor):
    owner, partner = [(jnp.arange(array.shape[axis_at]) // (array.shape[axis_at] // parts)).reshape([-1 if axis == axis_at else 1 for axis in range(array.ndim)]) for axis_at in (source, target)]
    chosen = jax.random.permutation(rng, parts)[partner]
    strong = (owner == chosen) | (owner == (partner + parts // 2) % parts)
    return jnp.where(strong, factor * array, array)


def block_levels(key, dims, shards, least, largest):
    factor_of, own = 1.0, jax.random.fold_in(key, 6)
    for axis_at, parts in shards:
        draws = jnp.exp(jax.random.uniform(jax.random.fold_in(own, axis_at), (parts,), jnp.float32, least / len(shards), largest / len(shards)))
        factor_of = factor_of * jnp.repeat(draws, dims[axis_at] // parts).reshape([-1 if axis == axis_at else 1 for axis in range(len(dims))])
    return factor_of


def normal_values(key, dims, spread, limit, cuts=(), dtype=jnp.bfloat16):
    result = spread * jax.random.normal(key, dims, jnp.float32)
    if cuts:
        result = result * block_levels(key, dims, cuts, -0.22, 0.18)
    return jnp.clip(result, -limit, limit).astype(dtype)


def bell_draw_with(own_key, extent, deviation, reach, split, heavy, held_as=jnp.bfloat16):
    drawn = deviation * jax.random.normal(own_key, extent, jnp.float32)
    if split:
        drawn = drawn * block_levels(own_key, extent, split, -0.22, 0.18)
    return jnp.clip(strengthened(drawn, jax.random.fold_in(own_key, 3), *heavy), -reach, reach).astype(held_as)


def setup_inputs(seed: int = 0) -> dict:
    keys = jax.random.split(jax.random.key(seed), 7)
    return {
        "features": bell_draw_with(keys[0], (TOKENS, D), 1.0, 8.0, ((0, 16), (1, 16)), (1, 0, 16, 2.0)),
        "w_in": normal_values(keys[1], (D, FF), D ** -0.5, 0.078125, ((0, 16), (1, 16))),
        "b_in": normal_values(keys[2], (FF,), 0.5, 3.0, ((0, 16),), jnp.float32),
        "w_out": normal_values(keys[3], (FF, D), FF ** -0.5, 0.0390625, ((0, 16), (1, 16))),
        "b_out": normal_values(keys[4], (D,), 0.5, 3.0, ((0, 16),), jnp.float32),
        "grad_out": normal_values(keys[5], (TOKENS, D), 1.0, 6.0, ((0, 16), (1, 16))),
    }


def rounded(value):
    return lax.optimization_barrier(value.astype(jnp.bfloat16)).astype(jnp.float32)

def gelu_parts(hidden):
    cdf = 0.5 * (1.0 + jax.scipy.special.erf(hidden * (1.0 / math.sqrt(2.0))))
    density = jnp.exp(-0.5 * hidden * hidden) * (1.0 / math.sqrt(2.0 * math.pi))
    return (hidden * cdf, cdf + hidden * density)

def reference(features, w_in, b_in, w_out, b_out, grad_out):
    feat_block = D // N_ROW
    hid_block = FF // N_COL
    hidden = jnp.zeros((TOKENS, FF), jnp.float32)
    for index in range(N_ROW):
        lower = index * feat_block
        hidden = hidden + rounded(jnp.dot(features[:, lower:lower + feat_block], w_in[lower:lower + feat_block], preferred_element_type=jnp.float32))
    hidden = hidden + b_in
    act_full, slopes = gelu_parts(hidden)
    act = act_full.astype(jnp.bfloat16)
    out_sum = jnp.zeros((TOKENS, D), jnp.float32)
    for index in range(N_COL):
        lower = index * hid_block
        out_sum = out_sum + rounded(jnp.dot(act[:, lower:lower + hid_block], w_out[lower:lower + hid_block], preferred_element_type=jnp.float32))
    branch_out = (out_sum + b_out).astype(jnp.bfloat16)
    grad_act = jnp.zeros((TOKENS, FF), jnp.float32)
    for index in range(N_ROW):
        lower = index * feat_block
        grad_act = grad_act + rounded(jnp.dot(grad_out[:, lower:lower + feat_block], w_out[:, lower:lower + feat_block].T, preferred_element_type=jnp.float32))
    grad_hidden = (grad_act * slopes).astype(jnp.bfloat16)
    grad_w_in = jnp.dot(features.T, grad_hidden, preferred_element_type=jnp.float32)
    grad_b_in = lax.optimization_barrier(jnp.sum(grad_hidden.astype(jnp.float32), axis=0))
    grad_w_out = jnp.dot(act.T, grad_out, preferred_element_type=jnp.float32)
    grad_b_out = lax.optimization_barrier(jnp.sum(grad_out.astype(jnp.float32), axis=0))
    grad_sum = jnp.zeros((TOKENS, D), jnp.float32)
    for index in range(N_COL):
        lower = index * hid_block
        grad_sum = grad_sum + rounded(jnp.dot(grad_hidden[:, lower:lower + hid_block], w_in[:, lower:lower + hid_block].T, preferred_element_type=jnp.float32))
    grad_features = grad_sum.astype(jnp.bfloat16)
    return (branch_out, grad_features, grad_w_in, grad_b_in, grad_w_out, grad_b_out)
```

```python
import math

import jax
import jax.numpy as jnp
from jax import lax
from jax.sharding import Mesh, PartitionSpec as P

BF16 = jnp.bfloat16
F32 = jnp.float32

Z, YL, YH, X, C = 8, 2, 2, 4, 2


def gelu_parts(hidden):
    cdf = 0.5 * (1.0 + jax.scipy.special.erf(hidden * (1.0 / math.sqrt(2.0))))
    density = jnp.exp(-0.5 * hidden * hidden) * (1.0 / math.sqrt(2.0 * math.pi))
    return (hidden * cdf, cdf + hidden * density)


def dot(left, right, left_dim, right_dim):
    return lax.dot_general(
        left, right, (((left_dim,), (right_dim,)), ((), ())), preferred_element_type=F32
    )


def flip_c(v):
    return lax.ppermute(v, "c", [(0, 1), (1, 0)])


def flip_yl(v):
    return lax.ppermute(v, "yl", [(0, 1), (1, 0)])


def flip_yh(v):
    return lax.ppermute(v, "yh", [(0, 1), (1, 0)])


def flip_both(v):
    return lax.ppermute(v, ("yl", "yh"), [(i, 3 - i) for i in range(4)])


def pair_x(v):
    return lax.ppermute(v, "x", [(i, i ^ 1) for i in range(X)])


def mirror_x(v):
    return lax.ppermute(v, "x", [(i, 3 - i) for i in range(X)])


def step_z(v, shift):
    return lax.ppermute(v, "z", [(i, (i + shift) % Z) for i in range(Z)])


def plane_gather(v):
    same = jnp.concatenate([v, flip_yl(v)], axis=1)
    other = jnp.concatenate([flip_yh(v), flip_both(v)], axis=1)
    t = v.shape[0]
    same = jnp.concatenate([same, pair_x(same)], axis=0)
    other_m = mirror_x(other)
    same = jnp.concatenate([same, mirror_x(same)], axis=0)
    two = jnp.concatenate([other, other_m], axis=0)
    two_p = pair_x(two)
    other = jnp.concatenate([other, two_p[:t], other_m, two_p[t:]], axis=0)
    mine = jnp.concatenate([same, other], axis=0)
    return jnp.concatenate([mine, flip_c(mine)], axis=0)


def plane_sums(term, t):
    half = 8 * t

    def plus(value, came):
        return value + came.astype(F32)

    came = flip_c(term(half, half).astype(BF16))
    mine = plus(term(0, half), came)
    same, other = mine[: 4 * t], mine[4 * t :]
    came = mirror_x(same[2 * t :].astype(BF16))
    same = plus(same[: 2 * t], came)
    came = pair_x(jnp.concatenate([other[t : 2 * t], other[3 * t :]], axis=0).astype(BF16))
    other = plus(jnp.concatenate([other[:t], other[2 * t : 3 * t]], axis=0), came)
    same = plus(same[:t], pair_x(same[t:].astype(BF16)))
    other = plus(other[:t], mirror_x(other[t:].astype(BF16)))
    d = same.shape[1] // 2
    total = same[:, :d]
    total = plus(total, flip_yl(same[:, d:].astype(BF16)))
    total = plus(total, flip_yh(other[:, :d].astype(BF16)))
    return plus(total, flip_both(other[:, d:].astype(BF16)))


def ring_sums(term, up_steps):
    down_steps = Z - 1 - up_steps
    up = down = None
    for s in range(max(up_steps, down_steps)):
        if s < up_steps:
            value = term(up_steps - s)
            up = step_z((value if up is None else value + up.astype(F32)).astype(BF16), 1)
        if s < down_steps:
            value = term(Z - (down_steps - s))
            down = step_z((value if down is None else value + down.astype(F32)).astype(BF16), -1)
    return term(0) + up.astype(F32) + down.astype(F32)


def ring_gather(own, position, up_steps):
    down_steps = Z - 1 - up_steps
    rows = own.shape[0]
    pieces = [(0, own)]
    up = down = own
    for s in range(max(up_steps, down_steps)):
        if s < up_steps:
            up = step_z(up, 1)
            pieces.append((Z - 1 - s, up))
        if s < down_steps:
            down = step_z(down, -1)
            pieces.append((1 + s, down))
    whole = jnp.zeros((Z * rows, own.shape[1]), own.dtype)
    for j, piece in pieces:
        whole = lax.dynamic_update_slice(whole, piece, ((position + j) % Z * rows, 0))
    return whole


def body(features, w_in, b_in, w_out, b_out, grad_out):
    position = lax.axis_index("z")
    side = lax.axis_index("yl")
    t, d = features.shape
    f = w_in.shape[1] // 2
    rows = 2 * t

    def my_half(array, axis, which):
        return lax.dynamic_slice_in_dim(array, which * f, f, axis)

    first = jnp.concatenate(
        [my_half(w_in, 1, side), flip_yl(my_half(w_in, 1, 1 - side))], axis=0
    )
    second = jnp.concatenate(
        [my_half(w_out, 0, side), flip_yl(my_half(w_out, 0, 1 - side))], axis=1
    )
    tokens = plane_gather(features)
    cotangent = plane_gather(grad_out)

    def chunk(array, j):
        return lax.dynamic_slice_in_dim(array, (position + j) % Z * rows, rows, 0)

    hidden = ring_sums(lambda j: dot(chunk(tokens, j), first, 1, 0), 3)
    grad_act = ring_sums(lambda j: dot(chunk(cotangent, j), second, 1, 1), 4)
    act, slopes = gelu_parts(hidden + my_half(b_in, 0, side))
    grad_hidden = (grad_act * slopes).astype(BF16)
    act = ring_gather(act.astype(BF16), position, 3)
    grad_hidden = ring_gather(grad_hidden, position, 4)

    branch_out = plane_sums(
        lambda begin, count: dot(act[begin : begin + count], second, 1, 0), t
    )
    branch_out = (branch_out + b_out).astype(BF16)
    grad_features = plane_sums(
        lambda begin, count: dot(grad_hidden[begin : begin + count], first, 1, 1), t
    ).astype(BF16)

    def both_halves(mine, partner, axis):
        partner = partner.astype(F32)
        return jnp.where(
            side == 0,
            jnp.concatenate([mine, partner], axis=axis),
            jnp.concatenate([partner, mine], axis=axis),
        )

    grad_w_in = dot(tokens, grad_hidden, 0, 0)
    grad_w_in = both_halves(grad_w_in[:d], flip_yl(grad_w_in[d:].astype(BF16)), 1)
    grad_w_out = dot(act, cotangent, 0, 0)
    grad_w_out = both_halves(grad_w_out[:, :d], flip_yl(grad_w_out[:, d:].astype(BF16)), 0)
    grad_b_in = jnp.sum(grad_hidden, axis=0, dtype=F32)
    grad_b_in = both_halves(grad_b_in, flip_yl(grad_b_in), 0)
    grad_b_out = jnp.sum(cotangent[:, :d], axis=0, dtype=F32)
    return (branch_out, grad_features, grad_w_in, grad_b_in, grad_w_out, grad_b_out)


def solution(mesh):
    fine = Mesh(mesh.devices.reshape(Z, YL, YH, X, C), ("z", "yl", "yh", "x", "c"))
    row, col = ("z", "yl"), ("yh", "x", "c")
    return jax.shard_map(
        body,
        mesh=fine,
        in_specs=(P(col, row), P(row, col), P(col), P(col, row), P(row), P(col, row)),
        out_specs=(P(col, row), P(col, row), P(row, col), P(col), P(col, row), P(row)),
        check_vma=False,
    )
```

```python
import math

import jax
import jax.numpy as jnp
from jax import lax
from jax.sharding import Mesh, PartitionSpec as P

BF16 = jnp.bfloat16
F32 = jnp.float32

Z, YL, YH, X, C = 8, 2, 2, 4, 2


def gelu_parts(hidden):
    cdf = 0.5 * (1.0 + jax.scipy.special.erf(hidden * (1.0 / math.sqrt(2.0))))
    density = jnp.exp(-0.5 * hidden * hidden) * (1.0 / math.sqrt(2.0 * math.pi))
    return (hidden * cdf, cdf + hidden * density)


def dot(left, right, left_dim, right_dim):
    return lax.dot_general(
        left, right, (((left_dim,), (right_dim,)), ((), ())), preferred_element_type=F32
    )


def flip_c(v):
    return lax.ppermute(v, "c", [(0, 1), (1, 0)])


def flip_yl(v):
    return lax.ppermute(v, "yl", [(0, 1), (1, 0)])


def flip_yh(v):
    return lax.ppermute(v, "yh", [(0, 1), (1, 0)])


def flip_both(v):
    return lax.ppermute(v, ("yl", "yh"), [(i, 3 - i) for i in range(4)])


def pair_x(v):
    return lax.ppermute(v, "x", [(i, i ^ 1) for i in range(X)])


def mirror_x(v):
    return lax.ppermute(v, "x", [(i, 3 - i) for i in range(X)])


def step_z(v, shift):
    return lax.ppermute(v, "z", [(i, (i + shift) % Z) for i in range(Z)])


def together(*values):
    return lax.optimization_barrier(values)


def after(value, *others):
    return together(value, *others)[0]


def beside(left, right):
    return jnp.concatenate([left, right], axis=1)


def far_tokens(same, other, same_p, other_m):
    t = same.shape[0]
    same = jnp.concatenate([same, same_p], axis=0)
    came, far = mirror_x(same), pair_x(jnp.concatenate([other, other_m], axis=0))

    def laid_out(came, far):
        return jnp.concatenate([same, came, other, far[:t], other_m, far[t:]], axis=0)

    return came, far, laid_out


def plane_sums(term, t, early=()):
    def plus(value, came):
        return value.astype(F32) + came.astype(F32)

    leave = term(2 * t, 2 * t), term(4 * t, 4 * t)
    came, far = mirror_x(leave[0]), leave[1]
    other = jnp.concatenate([far[:t], far[2 * t : 3 * t]], axis=0)
    far = pair_x(jnp.concatenate([far[t : 2 * t], far[3 * t :]], axis=0))
    same = term(0, 2 * t)
    came, far, *_ = together(came, far, *early)
    same = plus(same, came)
    other = plus(other, far)
    came, far = together(pair_x(same[t:].astype(BF16)), mirror_x(other[t:].astype(BF16)))
    same = plus(same[:t], came)
    other = plus(other[:t], far)
    middle = same, other
    d = same.shape[1] // 2
    near, over, both = together(
        flip_yl(same[:, d:].astype(BF16)),
        flip_yh(other[:, :d].astype(BF16)),
        flip_both(other[:, d:].astype(BF16)),
    )
    return plus(plus(plus(same[:, :d], near), over), both), leave, middle


def ring_sums(partial, position, up_steps):
    down_steps = Z - 1 - up_steps
    rows = partial.shape[0] // Z

    def term(j):
        return lax.dynamic_slice_in_dim(partial, (position + j) % Z * rows, rows, 0)

    def plus(value, came):
        return (value.astype(F32) + came.astype(F32)).astype(BF16)

    up, down = term(up_steps), term(Z - down_steps)
    for s in range(1, Z // 2 + 1):
        moved_up = step_z(up, 1) if s <= up_steps else up
        moved_down = step_z(down, -1) if s <= down_steps else down
        up, down = together(moved_up, moved_down)
        if s < up_steps:
            up = plus(term(up_steps - s), up)
        if s < down_steps:
            down = plus(term(Z - down_steps + s), down)
    return term(0).astype(F32) + up.astype(F32) + down.astype(F32)


def ring_gather(own, position, up_steps):
    down_steps = Z - 1 - up_steps
    rows = own.shape[0]
    pieces = [(0, own)]
    up = down = own
    for s in range(1, Z // 2 + 1):
        moved_up = step_z(up, 1) if s <= up_steps else up
        moved_down = step_z(down, -1) if s <= down_steps else down
        up, down = together(moved_up, moved_down)
        if s <= up_steps:
            pieces.append((Z - s, up))
        if s <= down_steps:
            pieces.append((s, down))
    whole = jnp.zeros((Z * rows, own.shape[1]), own.dtype)
    for j, piece in pieces:
        whole = lax.dynamic_update_slice(whole, piece, ((position + j) % Z * rows, 0))
    return whole


def body(features, w_in, b_in, w_out, b_out, grad_out):
    position = lax.axis_index("z")
    side = lax.axis_index("yl")
    t, d = features.shape
    f = w_in.shape[1] // 2

    def my_half(array, axis, which):
        return lax.dynamic_slice_in_dim(array, which * f, f, axis)

    def both_sides(mine, partner, axis):
        partner = partner.astype(F32)
        return jnp.where(
            side == 0,
            jnp.concatenate([mine, partner], axis=axis),
            jnp.concatenate([partner, mine], axis=axis),
        )

    near, over, both = together(flip_yl(features), flip_yh(features), flip_both(features))
    same, other = beside(features, near), beside(over, both)
    mine, sent = my_half(w_in, 1, side), my_half(w_in, 1, 1 - side)
    came_in = flip_yl(after(sent, near))
    same_p, other_m = together(pair_x(same), mirror_x(other))
    held = after(grad_out, same_p)
    near, over, both = flip_yl(held), flip_yh(held), flip_both(held)
    came, far, laid_out = far_tokens(same, other, same_p, other_m)
    came, far = together(came, far)
    tokens = laid_out(came, far)
    first = jnp.concatenate([mine, came_in], axis=0)
    first = jnp.concatenate([first, flip_c(first)], axis=1)
    partial = dot(tokens, first, 1, 0).astype(BF16)

    mine, sent = my_half(w_out, 0, side), my_half(w_out, 0, 1 - side)
    second = jnp.concatenate([mine, flip_yl(after(sent, came_in))], axis=1)
    second = jnp.concatenate([second, flip_c(second)], axis=0)
    same, other, _ = together(beside(held, near), beside(over, both), came)
    same_p, other_m, partial = together(pair_x(same), mirror_x(other), partial)
    came, far, laid_out = far_tokens(same, other, same_p, other_m)
    cotangent = laid_out(*together(came, far))
    grad_b_out = jnp.sum(cotangent[:, :d], axis=0, dtype=F32)
    bias = my_half(b_in, 0, side)
    came = flip_c(jnp.concatenate([bias, grad_b_out]))
    bias = jnp.concatenate([bias, came[:f]])
    grad_b_out = grad_b_out + came[f:]

    hidden = ring_sums(partial, position, 3)
    grad_act = ring_sums(dot(cotangent, second, 1, 1).astype(BF16), position, 4)
    act, slopes = gelu_parts(hidden + bias)
    grad_hidden = (grad_act * slopes).astype(BF16)
    act = ring_gather(act.astype(BF16), position, 3)
    grad_hidden = ring_gather(grad_hidden, position, 4)

    def rows_of(array, weight, right_dim):
        def term(begin, rows):
            return dot(array[begin : begin + rows], weight, 1, right_dim).astype(BF16)

        return term

    def over_cores(grad, axis):
        own = lax.slice_in_dim(grad, 0, f, axis=axis)
        sibling = lax.slice_in_dim(grad, f, 2 * f, axis=axis)
        return own + flip_c(sibling.astype(BF16)).astype(F32)

    branch_out, leave, middle = plane_sums(rows_of(act, second, 0), t)
    branch_out = (branch_out + b_out).astype(BF16)
    held = after(act, *leave)
    partner = over_cores(dot(held, cotangent[:, d:], 0, 0), 0)
    grad_w_out = over_cores(dot(held, cotangent[:, :d], 0, 0), 0)
    partner_out = flip_yl(partner.astype(BF16))

    grad_hidden = after(grad_hidden, partner, *middle)
    leave = dot(tokens[:, d:], grad_hidden, 0, 0)
    partner = flip_yl(over_cores(leave, 1).astype(BF16))
    held = after(grad_hidden, leave)
    grad_features, leave, _ = plane_sums(rows_of(held, first, 1), t, (partner_out,))
    grad_features = grad_features.astype(BF16)
    held = after(held, *leave)
    grad_w_in = over_cores(dot(tokens[:, :d], held, 0, 0), 1)
    grad_w_out = both_sides(grad_w_out, partner_out, 0)
    grad_w_in = both_sides(grad_w_in, partner, 1)
    grad_b_in = over_cores(jnp.sum(grad_hidden, axis=0, dtype=F32), 0)
    grad_b_in = both_sides(grad_b_in, flip_yl(grad_b_in), 0)
    return (branch_out, grad_features, grad_w_in, grad_b_in, grad_w_out, grad_b_out)


def solution(mesh):
    fine = Mesh(mesh.devices.reshape(Z, YL, YH, X, C), ("z", "yl", "yh", "x", "c"))
    row, col = ("z", "yl"), ("yh", "x", "c")
    return jax.shard_map(
        body,
        mesh=fine,
        in_specs=(P(col, row), P(row, col), P(col), P(col, row), P(row), P(col, row)),
        out_specs=(P(col, row), P(col, row), P(row, col), P(col), P(col, row), P(row)),
        check_vma=False,
    )
```

```python
import math

import jax
import jax.numpy as jnp
from jax import lax
from jax.sharding import Mesh, PartitionSpec as P

BF16 = jnp.bfloat16
F32 = jnp.float32

Z, YL, YH, X, C = 8, 2, 2, 4, 2


def gelu_parts(hidden):
    cdf = 0.5 * (1.0 + jax.scipy.special.erf(hidden * (1.0 / math.sqrt(2.0))))
    density = jnp.exp(-0.5 * hidden * hidden) * (1.0 / math.sqrt(2.0 * math.pi))
    return (hidden * cdf, cdf + hidden * density)


def dot(left, right, left_dim, right_dim):
    return lax.dot_general(
        left, right, (((left_dim,), (right_dim,)), ((), ())), preferred_element_type=F32
    )


def flip_c(v):
    return lax.ppermute(v, "c", [(0, 1), (1, 0)])


def flip_yl(v):
    return lax.ppermute(v, "yl", [(0, 1), (1, 0)])


def flip_yh(v):
    return lax.ppermute(v, "yh", [(0, 1), (1, 0)])


def flip_both(v):
    return lax.ppermute(v, ("yl", "yh"), [(i, 3 - i) for i in range(4)])


def pair_x(v):
    return lax.ppermute(v, "x", [(i, i ^ 1) for i in range(X)])


def mirror_x(v):
    return lax.ppermute(v, "x", [(i, 3 - i) for i in range(X)])


def step_z(v, shift):
    return lax.ppermute(v, "z", [(i, (i + shift) % Z) for i in range(Z)])


def together(*values):
    return lax.optimization_barrier(values)


def after(value, *others):
    return together(value, *others)[0]


def beside(left, right):
    return jnp.concatenate([left, right], axis=1)


def far_tokens(same, other, same_p, other_m):
    near = jnp.concatenate([same, same_p], axis=0), jnp.concatenate([other, other_m], axis=0)

    def laid_out(came, far):
        return jnp.concatenate([same, same_p, other, other_m, came, far], axis=0)

    return mirror_x(near[0]), pair_x(near[1]), laid_out


def plus(value, came):
    return value.astype(F32) + came.astype(F32)


def over_x(term, t, early=(), late=()):
    leave = term(4 * t, 2 * t), term(6 * t, 2 * t)
    came, far, *_ = together(mirror_x(leave[0]), pair_x(leave[1]), *early)
    held = term(0, 4 * t)
    same, other = plus(held[: 2 * t], came), plus(held[2 * t :], far)
    first = same, other
    came, far, *_ = together(pair_x(same[t:].astype(BF16)), mirror_x(other[t:].astype(BF16)), *late)
    return (plus(same[:t], came), plus(other[:t], far)), leave, first


def over_y(same, other):
    d = same.shape[1] // 2
    near, over, both = together(
        flip_yl(same[:, d:].astype(BF16)),
        flip_yh(other[:, :d].astype(BF16)),
        flip_both(other[:, d:].astype(BF16)),
    )
    return plus(plus(plus(same[:, :d], near), over), both)


def ring_sums(partial, position, up_steps):
    down_steps = Z - 1 - up_steps
    rows = partial.shape[0] // Z

    def term(j):
        return lax.dynamic_slice_in_dim(partial, (position + j) % Z * rows, rows, 0)

    def plus(value, came):
        return (value.astype(F32) + came.astype(F32)).astype(BF16)

    up, down = term(up_steps), term(Z - down_steps)
    for s in range(1, Z // 2 + 1):
        moved_up = step_z(up, 1) if s <= up_steps else up
        moved_down = step_z(down, -1) if s <= down_steps else down
        up, down = together(moved_up, moved_down)
        if s < up_steps:
            up = plus(term(up_steps - s), up)
        if s < down_steps:
            down = plus(term(Z - down_steps + s), down)
    return term(0).astype(F32) + up.astype(F32) + down.astype(F32)


def ring_gather(own, position, up_steps):
    down_steps = Z - 1 - up_steps
    rows = own.shape[0]
    pieces = [(0, own)]
    up = down = own
    for s in range(1, Z // 2 + 1):
        moved_up = step_z(up, 1) if s <= up_steps else up
        moved_down = step_z(down, -1) if s <= down_steps else down
        up, down = together(moved_up, moved_down)
        if s <= up_steps:
            pieces.append((Z - s, up))
        if s <= down_steps:
            pieces.append((s, down))
    whole = jnp.zeros((Z * rows, own.shape[1]), own.dtype)
    for j, piece in pieces:
        whole = lax.dynamic_update_slice(whole, piece, ((position + j) % Z * rows, 0))
    return whole


def body(features, w_in, b_in, w_out, b_out, grad_out):
    position = lax.axis_index("z")
    side = lax.axis_index("yl")
    t, d = features.shape
    f = w_in.shape[1] // 2

    def my_half(array, axis, which):
        return lax.dynamic_slice_in_dim(array, which * f, f, axis)

    def both_sides(mine, partner, axis):
        partner = partner.astype(F32)
        return jnp.where(
            side == 0,
            jnp.concatenate([mine, partner], axis=axis),
            jnp.concatenate([partner, mine], axis=axis),
        )

    near, over, both = together(flip_yl(features), flip_yh(features), flip_both(features))
    same, other = beside(features, near), beside(over, both)
    mine, sent = my_half(w_in, 1, side), my_half(w_in, 1, 1 - side)
    came_in = flip_yl(after(sent, near))
    same_p, other_m = together(pair_x(same), mirror_x(other))
    came, far, laid_out = far_tokens(same, other, same_p, other_m)
    came, far = together(came, far)
    tokens = laid_out(came, far)
    first = jnp.concatenate([mine, came_in], axis=0)
    first = jnp.concatenate([first, flip_c(first)], axis=1)
    partial = dot(tokens, first, 1, 0).astype(BF16)

    held = after(grad_out, same_p)
    near, over, both = together(flip_yl(held), flip_yh(held), flip_both(held))
    same, other = beside(held, near), beside(over, both)
    same_p, other_m, _ = together(pair_x(same), mirror_x(other), partial)
    came, far, laid_out = far_tokens(same, other, same_p, other_m)
    cotangent = laid_out(*together(came, far))
    mine, sent = my_half(w_out, 0, side), my_half(w_out, 0, 1 - side)
    came_out = flip_yl(after(sent, came_in))
    second = jnp.concatenate([mine, came_out], axis=1)
    second = jnp.concatenate([second, flip_c(second)], axis=0)
    grad_b_out = jnp.sum(cotangent[:, :d], axis=0, dtype=F32)
    bias = my_half(b_in, 0, side)
    came = flip_c(jnp.concatenate([bias, grad_b_out]))
    bias = jnp.concatenate([bias, came[:f]])
    grad_b_out = grad_b_out + came[f:]

    partial_grad = dot(cotangent, second, 1, 1).astype(BF16)
    hidden = ring_sums(partial, position, 3)
    grad_act = ring_sums(partial_grad, position, 4)
    act, slopes = gelu_parts(hidden + bias)
    grad_hidden = (grad_act * slopes).astype(BF16)
    act = ring_gather(act.astype(BF16), position, 3)
    grad_hidden = ring_gather(grad_hidden, position, 4)

    def rows_of(array, weight, right_dim):
        def term(begin, rows):
            return dot(array[begin : begin + rows], weight, 1, right_dim).astype(BF16)

        return term

    def over_cores(grad, axis):
        own = lax.slice_in_dim(grad, 0, f, axis=axis)
        sibling = lax.slice_in_dim(grad, f, 2 * f, axis=axis)
        return own + flip_c(sibling.astype(BF16)).astype(F32)

    out_blocks, leave, _ = over_x(rows_of(act, second, 0), t)
    held = after(act, *leave)
    partner_sum = over_cores(dot(held, cotangent[:, d:], 0, 0), 0)
    partner_out = flip_yl(partner_sum.astype(BF16))
    grad_w_out = over_cores(dot(held, cotangent[:, :d], 0, 0), 0)

    grad_hidden = after(grad_hidden, partner_sum, *out_blocks)
    par = dot(tokens[:, d:], grad_hidden, 0, 0)
    sums = jnp.sum(grad_hidden, axis=0, dtype=F32)[None, :]
    sums = jnp.concatenate([sums, jnp.zeros((15, 2 * f), F32)], axis=0)
    partner_in = over_cores(jnp.concatenate([par, sums], axis=0), 1)
    grad_b_in = partner_in[d]
    partner_in = partner_in.astype(BF16)
    q = f // 3
    partner = flip_yl(partner_in[:, :q])
    late = flip_yl(after(partner_in[:, q:], partner))
    held = after(grad_hidden, par)
    blocks, _, begun = over_x(rows_of(held, first, 1), t, (partner_out, partner), (late,))
    partner = beside(partner, late)
    held = after(held, *begun)
    grad_w_in = over_cores(dot(tokens[:, :d], held, 0, 0), 1)
    both_outs = over_y(
        *(jnp.concatenate(pair, axis=0) for pair in zip(out_blocks, blocks))
    )
    branch_out = (both_outs[:t] + b_out).astype(BF16)
    grad_features = both_outs[t:].astype(BF16)
    grad_w_out = both_sides(grad_w_out, partner_out, 0)
    grad_w_in = both_sides(grad_w_in, partner[:d], 1)
    grad_b_in = both_sides(grad_b_in, partner[d], 0)
    return (branch_out, grad_features, grad_w_in, grad_b_in, grad_w_out, grad_b_out)


def solution(mesh):
    fine = Mesh(mesh.devices.reshape(Z, YL, YH, X, C), ("z", "yl", "yh", "x", "c"))
    row, col = ("z", "yl"), ("yh", "x", "c")
    return jax.shard_map(
        body,
        mesh=fine,
        in_specs=(P(col, row), P(row, col), P(col), P(col, row), P(row), P(col, row)),
        out_specs=(P(col, row), P(col, row), P(row, col), P(col), P(col, row), P(row)),
        check_vma=False,
    )
```

```python
import math

import jax
import jax.numpy as jnp
from jax import lax
from jax.sharding import Mesh, PartitionSpec as P

BF16 = jnp.bfloat16
F32 = jnp.float32

Z, YL, YH, X, C = 8, 2, 2, 4, 2


def gelu_parts(hidden):
    cdf = 0.5 * (1.0 + jax.scipy.special.erf(hidden * (1.0 / math.sqrt(2.0))))
    density = jnp.exp(-0.5 * hidden * hidden) * (1.0 / math.sqrt(2.0 * math.pi))
    return (hidden * cdf, cdf + hidden * density)


def dot(left, right, left_dim, right_dim):
    return lax.dot_general(
        left, right, (((left_dim,), (right_dim,)), ((), ())), preferred_element_type=F32
    )


def flip_c(v):
    return lax.ppermute(v, "c", [(0, 1), (1, 0)])


def flip_yl(v):
    return lax.ppermute(v, "yl", [(0, 1), (1, 0)])


def flip_yh(v):
    return lax.ppermute(v, "yh", [(0, 1), (1, 0)])


def flip_both(v):
    return lax.ppermute(v, ("yl", "yh"), [(i, 3 - i) for i in range(4)])


def pair_x(v):
    return lax.ppermute(v, "x", [(i, i ^ 1) for i in range(X)])


def mirror_x(v):
    return lax.ppermute(v, "x", [(i, 3 - i) for i in range(X)])


def step_z(v, shift):
    return lax.ppermute(v, "z", [(i, (i + shift) % Z) for i in range(Z)])


def together(*values):
    return lax.optimization_barrier(values)


def after(value, *others):
    return together(value, *others)[0]


def beside(left, right):
    return jnp.concatenate([left, right], axis=1)


def far_tokens(same, other, same_p, other_m):
    near = jnp.concatenate([same, same_p], axis=0), jnp.concatenate([other, other_m], axis=0)

    def laid_out(came, far):
        return jnp.concatenate([same, same_p, other, other_m, came, far], axis=0)

    return mirror_x(near[0]), pair_x(near[1]), laid_out


def plus(value, came):
    return value.astype(F32) + came.astype(F32)


def over_x(term, t, early=(), late=()):
    leave = term(4 * t, 2 * t), term(6 * t, 2 * t)
    came, far, *_ = together(mirror_x(leave[0]), pair_x(leave[1]), *early)
    held = term(0, 4 * t)
    same, other = plus(held[: 2 * t], came), plus(held[2 * t :], far)
    first = same, other
    came, far, *_ = together(pair_x(same[t:].astype(BF16)), mirror_x(other[t:].astype(BF16)), *late)
    return (plus(same[:t], came), plus(other[:t], far)), leave, first


def over_y(same, other):
    d = same.shape[1] // 2
    near, over, both = together(
        flip_yl(same[:, d:].astype(BF16)),
        flip_yh(other[:, :d].astype(BF16)),
        flip_both(other[:, d:].astype(BF16)),
    )
    return plus(plus(plus(same[:, :d], near), over), both)


def ring_sums(partial, position, up_steps):
    down_steps = Z - 1 - up_steps
    rows = partial.shape[0] // Z

    def term(j):
        return lax.dynamic_slice_in_dim(partial, (position + j) % Z * rows, rows, 0)

    def plus(value, came):
        return (value.astype(F32) + came.astype(F32)).astype(BF16)

    up, down = term(up_steps), term(Z - down_steps)
    for s in range(1, Z // 2 + 1):
        moved_up = step_z(up, 1) if s <= up_steps else up
        moved_down = step_z(down, -1) if s <= down_steps else down
        up, down = together(moved_up, moved_down)
        if s < up_steps:
            up = plus(term(up_steps - s), up)
        if s < down_steps:
            down = plus(term(Z - down_steps + s), down)
    return term(0).astype(F32) + up.astype(F32) + down.astype(F32)


def ring_gather(own, position, up_steps):
    down_steps = Z - 1 - up_steps
    rows = own.shape[0]
    pieces = [(0, own)]
    up = down = own
    for s in range(1, Z // 2 + 1):
        moved_up = step_z(up, 1) if s <= up_steps else up
        moved_down = step_z(down, -1) if s <= down_steps else down
        up, down = together(moved_up, moved_down)
        if s <= up_steps:
            pieces.append((Z - s, up))
        if s <= down_steps:
            pieces.append((s, down))
    whole = jnp.zeros((Z * rows, own.shape[1]), own.dtype)
    for j, piece in pieces:
        whole = lax.dynamic_update_slice(whole, piece, ((position + j) % Z * rows, 0))
    return whole


def body(features, w_in, b_in, w_out, b_out, grad_out):
    position = lax.axis_index("z")
    side = lax.axis_index("yl")
    t, d = features.shape
    f = w_in.shape[1] // 2

    def my_half(array, axis, which):
        return lax.dynamic_slice_in_dim(array, which * f, f, axis)

    def both_sides(mine, partner, axis):
        partner = partner.astype(F32)
        return jnp.where(
            side == 0,
            jnp.concatenate([mine, partner], axis=axis),
            jnp.concatenate([partner, mine], axis=axis),
        )

    near, over, both = together(flip_yl(features), flip_yh(features), flip_both(features))
    same, other = beside(features, near), beside(over, both)
    mine, sent = my_half(w_in, 1, side), my_half(w_in, 1, 1 - side)
    came_in = flip_yl(after(sent, near))
    same_p, other_m = together(pair_x(same), mirror_x(other))
    came, far, laid_out = far_tokens(same, other, same_p, other_m)
    came, far = together(came, far)
    tokens = laid_out(came, far)
    first = jnp.concatenate([mine, came_in], axis=0)
    first = jnp.concatenate([first, flip_c(first)], axis=1)
    partial = dot(tokens, first, 1, 0).astype(BF16)

    held = after(grad_out, same_p)
    near, over, both = together(flip_yl(held), flip_yh(held), flip_both(held))
    same, other = beside(held, near), beside(over, both)
    hidden = ring_sums(partial, position, 3)
    same_p, other_m, _ = together(pair_x(same), mirror_x(other), partial)
    came, far, laid_out = far_tokens(same, other, same_p, other_m)
    cotangent = laid_out(*together(came, far))
    mine, sent = my_half(w_out, 0, side), my_half(w_out, 0, 1 - side)
    came_out = flip_yl(after(sent, came_in))
    second = jnp.concatenate([mine, came_out], axis=1)
    second = jnp.concatenate([second, flip_c(second)], axis=0)
    grad_b_out = jnp.sum(cotangent[:, :d], axis=0, dtype=F32)
    bias = my_half(b_in, 0, side)
    came = flip_c(jnp.concatenate([bias, grad_b_out]))
    bias = jnp.concatenate([bias, came[:f]])
    grad_b_out = grad_b_out + came[f:]

    partial_grad = dot(cotangent, second, 1, 1).astype(BF16)
    grad_act = ring_sums(partial_grad, position, 4)
    act, slopes = gelu_parts(hidden + bias)
    grad_hidden = (grad_act * slopes).astype(BF16)
    act = ring_gather(act.astype(BF16), position, 3)
    grad_hidden = ring_gather(grad_hidden, position, 4)

    def rows_of(array, weight, right_dim):
        def term(begin, rows):
            return dot(array[begin : begin + rows], weight, 1, right_dim).astype(BF16)

        return term

    def over_cores(grad, axis):
        own = lax.slice_in_dim(grad, 0, f, axis=axis)
        sibling = lax.slice_in_dim(grad, f, 2 * f, axis=axis)
        return own + flip_c(sibling.astype(BF16)).astype(F32)

    out_blocks, leave, _ = over_x(rows_of(act, second, 0), t)
    held = after(act, *leave)
    partner_sum = over_cores(dot(held, cotangent[:, d:], 0, 0), 0)
    partner_out = flip_yl(partner_sum.astype(BF16))
    grad_w_out = over_cores(dot(held, cotangent[:, :d], 0, 0), 0)

    grad_hidden = after(grad_hidden, partner_sum, *out_blocks)
    par = dot(tokens[:, d:], grad_hidden, 0, 0)
    sums = jnp.sum(grad_hidden, axis=0, dtype=F32)[None, :]
    sums = jnp.concatenate([sums, jnp.zeros((15, 2 * f), F32)], axis=0)
    partner_in = over_cores(jnp.concatenate([par, sums], axis=0), 1)
    grad_b_in = partner_in[d]
    partner_in = partner_in.astype(BF16)
    q = f // 3
    partner = flip_yl(partner_in[:, :q])
    late = flip_yl(after(partner_in[:, q:], partner))
    held = after(grad_hidden, par)
    blocks, _, begun = over_x(rows_of(held, first, 1), t, (partner_out, partner), (late,))
    partner = beside(partner, late)
    held = after(held, *begun)
    grad_w_in = over_cores(dot(tokens[:, :d], held, 0, 0), 1)
    both_outs = over_y(
        *(jnp.concatenate(pair, axis=0) for pair in zip(out_blocks, blocks))
    )
    branch_out = (both_outs[:t] + b_out).astype(BF16)
    grad_features = both_outs[t:].astype(BF16)
    grad_w_out = both_sides(grad_w_out, partner_out, 0)
    grad_w_in = both_sides(grad_w_in, partner[:d], 1)
    grad_b_in = both_sides(grad_b_in, partner[d], 0)
    return (branch_out, grad_features, grad_w_in, grad_b_in, grad_w_out, grad_b_out)


def solution(mesh):
    fine = Mesh(mesh.devices.reshape(Z, YL, YH, X, C), ("z", "yl", "yh", "x", "c"))
    row, col = ("z", "yl"), ("yh", "x", "c")
    return jax.shard_map(
        body,
        mesh=fine,
        in_specs=(P(col, row), P(row, col), P(col), P(col, row), P(row), P(col, row)),
        out_specs=(P(col, row), P(col, row), P(row, col), P(col), P(col, row), P(row)),
        check_vma=False,
    )
```
